32 devices in a mesh: grp: 1, outer: 32 (over z, y, x, core).
Axes of the slice: x: 2, y: 2, z: 4, core: 2. Of those that a mesh axis runs over, the one named last changes fastest.
Arguments:
- grad_out: bfloat16 [1024, 512, 128], P(('grp', 'outer')), may hold values from -6 to 6
- input_spec: bfloat16 [2, 1024, 512, 128], P(None, ('grp', 'outer')), may hold values from -6 to 6
- kernel_spec: bfloat16 [2, 1024, 512, 128], P(None, 'outer'), may hold values from -6 to 6
- filter_hidden: bfloat16 [1024, 512, 64], P('outer'), may hold values from -6 to 6
- filter_w: bfloat16 [64, 128], replicated, may hold values from -0.75 to 0.75
- decay: float32 [128], replicated, may hold values from 0.3 to 30
Outputs:
- grad_input: bfloat16 [1024, 512, 128], P(('grp', 'outer'))
- grad_filter_w: float32 [64, 128], P('grp')
- grad_decay: float32 [128], P('grp')
The draws below stay inside these ranges and needn't reach their ends.
All inputs are finite; a program needn't handle non-finite values.
Results may differ from the reference program's by a relative error of at most 0.0091.
Values may be sent and summed in bfloat16 or wider, within the bound.
A program may use at most 192 MiB of HBM per device.

```python
import math
import jax
import jax.numpy as jnp
from jax import lax

OUTER_F = 1024
INNER_F = 512
CHANNELS = 128
ORDER = 64
SEQ = 524288


def level_of(key, extent, shards, low, high):
    loudness, own = 1.0, jax.random.fold_in(key, 6)
    for axis_at, blocks in shards:
        steps = jnp.exp(jax.random.uniform(jax.random.fold_in(own, axis_at), (blocks,), jnp.float32, low / len(shards), high / len(shards)))
        loudness = loudness * jnp.repeat(steps, extent[axis_at] // blocks).reshape([-1 if axis == axis_at else 1 for axis in range(len(extent))])
    return loudness


def gaussian(own_key, extent, deviation, most, pieces=(), held_as=jnp.bfloat16):
    values = jax.random.normal(own_key, extent, jnp.float32) * deviation
    if len(pieces) > 0:
        values = level_of(own_key, extent, pieces, -0.22, 0.18) * values
    return jnp.clip(values, min=-most, max=most).astype(held_as)


def setup_inputs(seed: int = 0, part: int = 0) -> dict:
    splits = jax.random.split(jax.random.key(seed), 7)
    part_splits = jax.random.split(jax.random.fold_in(splits[6], part), 7)
    grad_out = gaussian(part_splits[0], (OUTER_F, INNER_F, CHANNELS), 1.0, 6.0, ((0, 32),))
    input_spec = gaussian(part_splits[1], (2, OUTER_F, INNER_F, CHANNELS), 1.0, 6.0, ((1, 32),))
    kernel_spec = gaussian(splits[2], (2, OUTER_F, INNER_F, CHANNELS), 1.0, 6.0, ((1, 32),))
    filter_hidden = gaussian(splits[3], (OUTER_F, INNER_F, ORDER), 1.0, 6.0, ((0, 32),))
    filter_w = gaussian(splits[4], (ORDER, CHANNELS), ORDER ** -0.5, 0.75)
    decay = jnp.clip(jnp.exp(jax.random.uniform(splits[5], (CHANNELS,), jnp.float32, math.log(0.3), math.log(30.0))), 0.3, 30.0)
    return {"grad_out": grad_out, "input_spec": input_spec, "kernel_spec": kernel_spec, "filter_hidden": filter_hidden, "filter_w": filter_w, "decay": decay}


def to_half(values):
    return lax.optimization_barrier(values.astype(jnp.bfloat16)).astype(jnp.float32)

def cos_sin(length):
    numbers = jnp.arange(length, dtype=jnp.int32)
    product = numbers[:, None] * numbers[None, :] % length
    angles = product.astype(jnp.float32) * (2.0 * math.pi / length)
    return (to_half(jnp.cos(angles)), to_half(jnp.sin(angles)))

def twiddle(freq_numbers, time_numbers, seq_len):
    product = freq_numbers[:, None] * time_numbers[None, :] % seq_len
    angles = product.astype(jnp.float32) * (2.0 * math.pi / seq_len)
    return (jnp.cos(angles)[:, :, None], jnp.sin(angles)[:, :, None])

def outer_section(matrix, values):
    full_shape = values.shape
    flattened = values.reshape(full_shape[0], -1)
    return jnp.dot(matrix, flattened, precision=lax.Precision.HIGHEST).reshape(full_shape)

def inner_section(values, matrix):
    return jnp.einsum('cbh,bd->cdh', values, matrix, precision=lax.Precision.HIGHEST)

def reference(grad_out, input_spec, kernel_spec, filter_hidden, filter_w, decay):
    cosine_outer, sine_outer = cos_sin(OUTER_F)
    cosine_inner, sine_inner = cos_sin(INNER_F)
    twist_cos, twist_sin = twiddle(jnp.arange(OUTER_F, dtype=jnp.int32), jnp.arange(INNER_F, dtype=jnp.int32), SEQ)
    inv_total = 1.0 / SEQ
    inv_root = 1.0 / math.sqrt(SEQ)
    row_numbers = jnp.arange(OUTER_F, dtype=jnp.int32)
    col_numbers = jnp.arange(INNER_F, dtype=jnp.int32)
    positions = (row_numbers[:, None] * INNER_F + col_numbers[None, :]).astype(jnp.float32) * inv_total
    hidden = filter_hidden.astype(jnp.float32)
    channel_block = min(16, CHANNELS)

    def one_block(offset):

        def take(array, axis_number):
            return lax.dynamic_slice_in_dim(array, offset, channel_block, axis_number).astype(jnp.float32)
        grad_block = take(grad_out, 2)
        part_real = outer_section(cosine_outer, grad_block)
        part_imag = -outer_section(sine_outer, grad_block)
        shifted_real = to_half(part_real * twist_cos + part_imag * twist_sin)
        shifted_imag = to_half(part_imag * twist_cos - part_real * twist_sin)
        spec_real = inner_section(shifted_real, cosine_inner) + inner_section(shifted_imag, sine_inner)
        spec_imag = inner_section(shifted_imag, cosine_inner) - inner_section(shifted_real, sine_inner)

        def correlate(spectrum):
            real_part = take(spectrum[0], 2)
            imag_part = take(spectrum[1], 2)
            return (to_half(real_part * spec_real + imag_part * spec_imag), to_half(real_part * spec_imag - imag_part * spec_real))

        def inverse(halves):
            real_part, imag_part = halves
            mixed_real = inner_section(real_part, cosine_inner) - inner_section(imag_part, sine_inner)
            mixed_imag = inner_section(imag_part, cosine_inner) + inner_section(real_part, sine_inner)
            turned_real = to_half(mixed_real * twist_cos - mixed_imag * twist_sin)
            turned_imag = to_half(mixed_imag * twist_cos + mixed_real * twist_sin)
            summed = outer_section(cosine_outer, turned_real) - outer_section(sine_outer, turned_imag)
            return (summed * inv_total).astype(jnp.bfloat16)
        grad_block_input = inverse(correlate(kernel_spec))
        grad_kernel = inverse(correlate(input_spec))
        kernel_values = grad_kernel.astype(jnp.float32)
        decay_block = take(decay, 0)
        window = jnp.exp(-decay_block * positions[:, :, None])
        raw_filter = jnp.einsum('abf,fh->abh', hidden, take(filter_w, 1), precision=lax.Precision.HIGHEST)
        scaled = to_half(kernel_values * window * inv_root)
        weight_block = jnp.einsum('abf,abh->fh', hidden, scaled, precision=lax.Precision.HIGHEST)
        decay_grad = -lax.optimization_barrier(jnp.sum(positions[:, :, None] * window * raw_filter * kernel_values, axis=(0, 1))) * inv_root
        return (grad_block_input, weight_block, decay_grad)
    offsets = jnp.arange(CHANNELS // channel_block, dtype=jnp.int32) * channel_block
    inputs_grad, weights_grad, decays_grad = lax.map(one_block, offsets)
    grad_input = jnp.moveaxis(inputs_grad, 0, 2).reshape(OUTER_F, INNER_F, CHANNELS)
    grad_filter_w = jnp.moveaxis(weights_grad, 0, 1).reshape(ORDER, CHANNELS)
    grad_decay = decays_grad.reshape(CHANNELS)
    return (grad_input, grad_filter_w, grad_decay)
```

```python
import functools
import math

import jax
import jax.numpy as jnp
from jax import lax
from jax.experimental import pallas as pl
from jax.experimental.pallas import tpu as pltpu
from jax.sharding import PartitionSpec as P

VMEM_BYTES = 56 * 1024 * 1024
PAIR = 2
ROWS = 4


def cos_sin(length):
    numbers = jnp.arange(length, dtype=jnp.int32)
    product = numbers[:, None] * numbers[None, :] % length
    angles = product.astype(jnp.float32) * (2.0 * math.pi / length)
    return (jnp.cos(angles).astype(jnp.bfloat16), jnp.sin(angles).astype(jnp.bfloat16))


def twiddle(freq_numbers, time_numbers, seq_len):
    product = freq_numbers[:, None] * time_numbers[None, :] % seq_len
    angles = product.astype(jnp.float32) * (2.0 * math.pi / seq_len)
    return (jnp.cos(angles)[:, :, None], jnp.sin(angles)[:, :, None])


def outer_section(matrix, values):
    full_shape = values.shape
    flattened = values.reshape(full_shape[0], -1)
    return jnp.dot(matrix, flattened, preferred_element_type=jnp.float32).reshape(full_shape)


def inner_section(values, matrix):
    return jnp.einsum("cbh,bd->cdh", values, matrix, preferred_element_type=jnp.float32)


def plain_shards(grad_out, input_spec, kernel_spec, filter_hidden, filter_w, decay):
    devices = lax.axis_size("outer")
    my_index = lax.axis_index("outer")
    rows_dev = grad_out.shape[0]
    inner_len = grad_out.shape[1]
    outer_len = rows_dev * devices
    seq_len = outer_len * inner_len
    cols_dev = inner_len // devices
    freq_dev = input_spec.shape[1]
    inv_total = 1.0 / seq_len
    inv_root = 1.0 / math.sqrt(seq_len)
    cosine_outer, sine_outer = cos_sin(outer_len)
    cosine_inner, sine_inner = cos_sin(inner_len)
    my_rows = my_index * rows_dev + jnp.arange(rows_dev, dtype=jnp.int32)
    row_positions = (
        my_rows[:, None] * inner_len + jnp.arange(inner_len, dtype=jnp.int32)[None, :]
    ).astype(jnp.float32) * inv_total
    columns = lax.all_to_all(grad_out, "outer", split_axis=1, concat_axis=0, tiled=True)
    part_real = outer_section(cosine_outer, columns)
    part_imag = -outer_section(sine_outer, columns)
    my_cols = my_index * cols_dev + jnp.arange(cols_dev, dtype=jnp.int32)
    twist_cos, twist_sin = twiddle(jnp.arange(outer_len, dtype=jnp.int32), my_cols, seq_len)
    shifted_real = (part_real * twist_cos + part_imag * twist_sin).astype(jnp.bfloat16)
    shifted_imag = (part_imag * twist_cos - part_real * twist_sin).astype(jnp.bfloat16)
    freq_real, freq_imag = (
        lax.all_to_all(shifted_real, "outer", split_axis=0, concat_axis=1, tiled=True),
        lax.all_to_all(shifted_imag, "outer", split_axis=0, concat_axis=1, tiled=True),
    )
    spec_real = inner_section(freq_real, cosine_inner) + inner_section(freq_imag, sine_inner)
    spec_imag = inner_section(freq_imag, cosine_inner) - inner_section(freq_real, sine_inner)
    my_freq = my_index * freq_dev + jnp.arange(freq_dev, dtype=jnp.int32)
    back_cos, back_sin = twiddle(my_freq, jnp.arange(inner_len, dtype=jnp.int32), seq_len)

    def correlate(spectrum):
        real_part = spectrum[0].astype(jnp.float32)
        imag_part = spectrum[1].astype(jnp.float32)
        return (
            (real_part * spec_real + imag_part * spec_imag).astype(jnp.bfloat16),
            (real_part * spec_imag - imag_part * spec_real).astype(jnp.bfloat16),
        )

    def inverse_inner(halves):
        real_part, imag_part = halves
        mixed_real = inner_section(real_part, cosine_inner) - inner_section(imag_part, sine_inner)
        mixed_imag = inner_section(imag_part, cosine_inner) + inner_section(real_part, sine_inner)
        return (
            (mixed_real * back_cos - mixed_imag * back_sin).astype(jnp.bfloat16),
            (mixed_imag * back_cos + mixed_real * back_sin).astype(jnp.bfloat16),
        )

    def last_section(real_part, imag_part):
        summed = outer_section(cosine_outer, real_part) - outer_section(sine_outer, imag_part)
        return (summed * inv_total).astype(jnp.bfloat16)

    def one_last(halves):
        return last_section(halves[0], halves[1])

    input_turned = inverse_inner(correlate(kernel_spec))
    grad_cols = one_last(
        (
            lax.all_to_all(input_turned[0], "outer", split_axis=1, concat_axis=0, tiled=True),
            lax.all_to_all(input_turned[1], "outer", split_axis=1, concat_axis=0, tiled=True),
        )
    )
    kernel_turned = inverse_inner(correlate(input_spec))
    kern_cols = one_last(
        (
            lax.all_to_all(kernel_turned[0], "outer", split_axis=1, concat_axis=0, tiled=True),
            lax.all_to_all(kernel_turned[1], "outer", split_axis=1, concat_axis=0, tiled=True),
        )
    )
    grad_rows, kern_here = (
        lax.all_to_all(grad_cols, "outer", split_axis=0, concat_axis=1, tiled=True),
        lax.all_to_all(kern_cols, "outer", split_axis=0, concat_axis=1, tiled=True),
    )
    kernel_values = kern_here.astype(jnp.float32)
    window = jnp.exp(-decay * row_positions[:, :, None])
    raw_filter = jnp.einsum(
        "abf,fh->abh", filter_hidden, filter_w, preferred_element_type=jnp.float32
    )
    scaled = (kernel_values * window * inv_root).astype(jnp.bfloat16)
    weight_part = jnp.einsum(
        "abf,abh->fh", filter_hidden, scaled, preferred_element_type=jnp.float32
    )
    decay_part = (
        -jnp.sum(row_positions[:, :, None] * window * raw_filter * kernel_values, axis=(0, 1))
        * inv_root
    )
    grad_filter_w, grad_decay = lax.psum((weight_part, decay_part), "outer")
    return (grad_rows, grad_filter_w, grad_decay)


def dot(matrix, values):
    return jnp.dot(matrix, values, preferred_element_type=jnp.float32)


def beside(blocks):
    return jnp.concatenate(blocks, axis=1)


def call(kernel, grid, in_specs, out_specs, out_shape, flops, moved, *operands):
    return pl.pallas_call(
        kernel,
        grid=(grid,),
        in_specs=in_specs,
        out_specs=out_specs,
        out_shape=out_shape,
        compiler_params=pltpu.CompilerParams(
            dimension_semantics=("arbitrary",), vmem_limit_bytes=VMEM_BYTES
        ),
        cost_estimate=pl.CostEstimate(flops=flops, bytes_accessed=moved, transcendentals=0),
    )(*operands)


def whole(array):
    zeros = (0,) * array.ndim
    return pl.BlockSpec(array.shape, lambda step: zeros)


def block(array, axis, size):
    shape = array.shape[:axis] + (size,) + array.shape[axis + 1 :]
    return pl.BlockSpec(
        shape, lambda step: tuple(step if at == axis else 0 for at in range(len(shape)))
    )


def outer_forward_kernel(cos_ref, sin_ref, tc_ref, ts_ref, x_ref, real_ref, imag_ref):
    lanes = x_ref.shape[-1]
    values = beside([x_ref[:, k].reshape(-1, lanes) for k in range(PAIR)])
    real = dot(cos_ref[...], values)
    imag = -dot(sin_ref[...], values)
    for k in range(PAIR):
        r = real[:, k * lanes : (k + 1) * lanes]
        i = imag[:, k * lanes : (k + 1) * lanes]
        real_ref[k] = (r * tc_ref[k] + i * ts_ref[k]).astype(jnp.bfloat16)
        imag_ref[k] = (i * tc_ref[k] - r * ts_ref[k]).astype(jnp.bfloat16)


def inner_kernel(cos_ref, sin_ref, tc_ref, ts_ref, fr_ref, fi_ref, s_ref, real_ref, imag_ref):
    lanes = fr_ref.shape[-1]
    cosine, sine = cos_ref[...], sin_ref[...]
    in_real = beside([fr_ref[:, k].reshape(-1, lanes) for k in range(ROWS)])
    in_imag = beside([fi_ref[:, k].reshape(-1, lanes) for k in range(ROWS)])
    spec_real = dot(cosine, in_real) + dot(sine, in_imag)
    spec_imag = dot(cosine, in_imag) - dot(sine, in_real)
    kept_real = beside([s_ref[0, k] for k in range(ROWS)]).astype(jnp.float32)
    kept_imag = beside([s_ref[1, k] for k in range(ROWS)]).astype(jnp.float32)
    corr_real = (kept_real * spec_real + kept_imag * spec_imag).astype(jnp.bfloat16)
    corr_imag = (kept_real * spec_imag - kept_imag * spec_real).astype(jnp.bfloat16)
    mixed_real = dot(cosine, corr_real) - dot(sine, corr_imag)
    mixed_imag = dot(cosine, corr_imag) + dot(sine, corr_real)
    out_shape = (real_ref.shape[0],) + real_ref.shape[2:]
    for k in range(ROWS):
        r = mixed_real[:, k * lanes : (k + 1) * lanes]
        i = mixed_imag[:, k * lanes : (k + 1) * lanes]
        turned_real = (r * tc_ref[k] - i * ts_ref[k]).astype(jnp.bfloat16)
        turned_imag = (i * tc_ref[k] + r * ts_ref[k]).astype(jnp.bfloat16)
        real_ref[:, k] = turned_real.reshape(out_shape)
        imag_ref[:, k] = turned_imag.reshape(out_shape)


def outer_inverse_kernel(inv_total, cos_ref, sin_ref, tr_ref, ti_ref, out_ref):
    lanes = tr_ref.shape[-1]
    real = beside([tr_ref[k] for k in range(PAIR)])
    imag = beside([ti_ref[k] for k in range(PAIR)])
    summed = (dot(cos_ref[...], real) - dot(sin_ref[...], imag)) * inv_total
    for k in range(PAIR):
        out_ref[k] = summed[:, k * lanes : (k + 1) * lanes].astype(jnp.bfloat16)


def filter_kernel(
    inner_len,
    inv_total,
    inv_root,
    first_ref,
    cos_ref,
    sin_ref,
    tr_ref,
    ti_ref,
    hidden_ref,
    w_ref,
    decay_ref,
    weight_ref,
    slope_ref,
):
    step = pl.program_id(0)

    @pl.when(step == 0)
    def _():
        weight_ref[...] = jnp.zeros_like(weight_ref)
        slope_ref[...] = jnp.zeros_like(slope_ref)

    lanes = tr_ref.shape[-1]
    real = beside([tr_ref[k] for k in range(PAIR)])
    imag = beside([ti_ref[k] for k in range(PAIR)])
    values = (dot(cos_ref[...], real) - dot(sin_ref[...], imag)) * inv_total
    shape = values.shape
    hidden = hidden_ref[:, 0].reshape(shape[0], hidden_ref.shape[-1])
    row = lax.broadcasted_iota(jnp.int32, shape, 0)
    lane = lax.broadcasted_iota(jnp.int32, shape, 1)
    column = first_ref[0] + PAIR * step + (lane >= lanes).astype(jnp.int32)
    position = (row * inner_len + column).astype(jnp.float32) * inv_total
    weighted = jnp.exp(-decay_ref[...] * position) * values
    raw_filter = dot(hidden, w_ref[...])
    slope = position * weighted * raw_filter
    slope_ref[...] += jnp.sum(slope.reshape(-1, 8, shape[1]), axis=0)
    scaled = (weighted * inv_root).astype(jnp.bfloat16)
    weight_ref[...] += lax.dot_general(
        hidden, scaled, (((0,), (0,)), ((), ())), preferred_element_type=jnp.float32
    )


def shards(grad_out, input_spec, kernel_spec, filter_hidden, filter_w, decay):
    devices = lax.axis_size("outer")
    my_index = lax.axis_index("outer")
    rows_dev, inner_len, lanes = grad_out.shape
    outer_len = rows_dev * devices
    seq_len = outer_len * inner_len
    cols_dev = inner_len // devices
    if rows_dev % 16 or cols_dev % 16 or devices % 2 or devices & (devices - 1):
        return plain_shards(
            grad_out, input_spec, kernel_spec, filter_hidden, filter_w, decay
        )
    freq_dev = input_spec.shape[1]
    half = devices // 2
    half_cols = inner_len // half
    half_len = freq_dev * half
    order = filter_hidden.shape[-1]
    inv_total = 1.0 / seq_len
    inv_root = 1.0 / math.sqrt(seq_len)
    groups = [list(range(half)), list(range(half, devices))]
    bf16 = functools.partial(jax.ShapeDtypeStruct, dtype=jnp.bfloat16)
    f32 = functools.partial(jax.ShapeDtypeStruct, dtype=jnp.float32)
    cosine_outer, sine_outer = cos_sin(outer_len)
    cosine_inner, sine_inner = cos_sin(inner_len)

    def exchange(values, axis_index_groups=None):
        return lax.all_to_all(
            values,
            "outer",
            split_axis=0,
            concat_axis=0,
            axis_index_groups=axis_index_groups,
            tiled=True,
        )

    columns = exchange(
        grad_out.reshape(rows_dev, devices, cols_dev, lanes).transpose(1, 2, 0, 3)
    )
    hidden = filter_hidden.reshape(rows_dev, half, half_cols // PAIR, PAIR * order)
    hidden = hidden.transpose(1, 2, 0, 3)
    hidden = jnp.concatenate((hidden, hidden), axis=0)
    hidden, columns = lax.optimization_barrier((hidden, columns))
    hidden = exchange(hidden)

    my_cols = my_index * cols_dev + jnp.arange(cols_dev, dtype=jnp.int32)
    twist_cos, twist_sin = twiddle(my_cols, jnp.arange(outer_len, dtype=jnp.int32), seq_len)
    table_bytes = 4 * outer_len * outer_len
    column_bytes = 2 * outer_len * cols_dev * lanes
    turn_bytes = 8 * 128 * outer_len * cols_dev
    outer_flops = 4 * outer_len * outer_len * cols_dev * lanes
    inner_flops = 16 * freq_dev * inner_len * inner_len * lanes
    shape = (cols_dev, outer_len, lanes)
    shifted = call(
        outer_forward_kernel,
        cols_dev // PAIR,
        [whole(cosine_outer), whole(sine_outer), block(twist_cos, 0, PAIR),
         block(twist_sin, 0, PAIR), block(columns, 1, PAIR)],
        [block(bf16(shape), 0, PAIR)] * 2,
        [bf16(shape)] * 2,
        outer_flops,
        table_bytes + 3 * column_bytes + turn_bytes,
        cosine_outer, sine_outer, twist_cos, twist_sin, columns,
    )
    freq_real, freq_imag = [
        exchange(part.reshape(cols_dev, devices, freq_dev, lanes).transpose(1, 2, 0, 3))
        for part in shifted
    ]
    my_freq = my_index * freq_dev + jnp.arange(freq_dev, dtype=jnp.int32)
    back_cos, back_sin = twiddle(my_freq, jnp.arange(inner_len, dtype=jnp.int32), seq_len)

    def turned_of(spectrum, freq_real, freq_imag, pieces):
        shape = (pieces, freq_dev, inner_len // pieces, lanes)
        return call(
            inner_kernel,
            freq_dev // ROWS,
            [whole(cosine_inner), whole(sine_inner), block(back_cos, 0, ROWS),
             block(back_sin, 0, ROWS), block(freq_real, 1, ROWS), block(freq_imag, 1, ROWS),
             block(spectrum, 1, ROWS)],
            [block(bf16(shape), 1, ROWS)] * 2,
            [bf16(shape)] * 2,
            inner_flops,
            6 * column_bytes + turn_bytes,
            cosine_inner, sine_inner, back_cos, back_sin, freq_real, freq_imag, spectrum,
        )

    def by_column(part):
        return part.transpose(2, 0, 1, 3).reshape(part.shape[2], -1, lanes)

    input_turned = turned_of(kernel_spec, freq_real, freq_imag, devices)
    (freq_real, freq_imag), input_turned = lax.optimization_barrier(
        ((freq_real, freq_imag), input_turned)
    )
    kernel_turned = turned_of(input_spec, freq_real, freq_imag, half)
    input_parts = [by_column(exchange(part)) for part in input_turned]
    kernel_parts = [exchange(part, groups) for part in kernel_turned]

    grad_cols = call(
        functools.partial(outer_inverse_kernel, inv_total),
        cols_dev // PAIR,
        [whole(cosine_outer), whole(sine_outer)] + [block(input_parts[0], 0, PAIR)] * 2,
        block(bf16(shape), 0, PAIR),
        bf16(shape),
        outer_flops,
        table_bytes + 3 * column_bytes,
        cosine_outer, sine_outer, *input_parts,
    )
    grad_cols = grad_cols.reshape(cols_dev, devices, rows_dev, lanes).transpose(1, 2, 0, 3)
    kernel_parts, grad_cols = lax.optimization_barrier((kernel_parts, grad_cols))
    grad_rows = exchange(grad_cols).transpose(1, 0, 2, 3).reshape(grad_out.shape)

    kernel_parts = [by_column(part) for part in kernel_parts]
    half_at = my_index // half * half_len
    half_cos = lax.dynamic_slice_in_dim(cosine_outer, half_at, half_len, 1)
    half_sin = lax.dynamic_slice_in_dim(sine_outer, half_at, half_len, 1)
    first = (my_index % half * half_cols).astype(jnp.int32).reshape(1)
    nothing = jnp.zeros_like(filter_w)
    paired_w = jnp.concatenate(
        (
            jnp.concatenate((filter_w, nothing), axis=1),
            jnp.concatenate((nothing, filter_w), axis=1),
        ),
        axis=0,
    )
    paired_decay = jnp.concatenate((decay, decay))[None]
    weight_shape, slope_shape = (PAIR * order, PAIR * lanes), (8, PAIR * lanes)
    weight, slope = call(
        functools.partial(filter_kernel, inner_len, inv_total, inv_root),
        half_cols // PAIR,
        [pl.BlockSpec(memory_space=pltpu.SMEM), whole(half_cos), whole(half_sin),
         block(kernel_parts[0], 0, PAIR), block(kernel_parts[1], 0, PAIR), block(hidden, 1, 1),
         whole(paired_w), whole(paired_decay)],
        [whole(f32(weight_shape)), whole(f32(slope_shape))],
        [f32(weight_shape), f32(slope_shape)],
        outer_flops,
        table_bytes // 2 + 3 * column_bytes,
        first, half_cos, half_sin, *kernel_parts, hidden, paired_w, paired_decay,
    )
    weight = weight[:order, :lanes] + weight[order:, lanes:]
    slope = jnp.sum(slope[:, :lanes] + slope[:, lanes:], axis=0, keepdims=True)
    both = jnp.concatenate((weight, -slope * inv_root), axis=0)
    step = 1
    while step < devices:
        pairs = [(source, source ^ step) for source in range(devices)]
        both = both + lax.ppermute(both, "outer", pairs)
        step *= 2
    return (grad_rows, both[:order], both[order])


def solution(mesh):
    placed = (
        P(("grp", "outer"), None, None),
        P(None, ("grp", "outer"), None, None),
        P(None, "outer", None, None),
        P("outer", None, None),
        P(),
        P(),
    )
    return jax.shard_map(
        shards,
        mesh=mesh,
        in_specs=placed,
        out_specs=(P(("grp", "outer"), None, None), P("grp", None), P("grp")),
        check_vma=False,
    )
```

```python
import functools
import math

import jax
import jax.numpy as jnp
from jax import lax
from jax.experimental import pallas as pl
from jax.experimental.pallas import tpu as pltpu
from jax.sharding import PartitionSpec as P

VMEM_BYTES = 56 * 1024 * 1024
PAIR = 2
ROWS = 4


def cos_sin(length):
    numbers = jnp.arange(length, dtype=jnp.int32)
    product = numbers[:, None] * numbers[None, :] % length
    angles = product.astype(jnp.float32) * (2.0 * math.pi / length)
    return (jnp.cos(angles).astype(jnp.bfloat16), jnp.sin(angles).astype(jnp.bfloat16))


def twiddle(freq_numbers, time_numbers, seq_len):
    product = freq_numbers[:, None] * time_numbers[None, :] % seq_len
    angles = product.astype(jnp.float32) * (2.0 * math.pi / seq_len)
    return (jnp.cos(angles)[:, :, None], jnp.sin(angles)[:, :, None])


def outer_section(matrix, values):
    full_shape = values.shape
    flattened = values.reshape(full_shape[0], -1)
    return jnp.dot(matrix, flattened, preferred_element_type=jnp.float32).reshape(full_shape)


def inner_section(values, matrix):
    return jnp.einsum("cbh,bd->cdh", values, matrix, preferred_element_type=jnp.float32)


def plain_shards(grad_out, input_spec, kernel_spec, filter_hidden, filter_w, decay):
    devices = lax.axis_size("outer")
    my_index = lax.axis_index("outer")
    rows_dev = grad_out.shape[0]
    inner_len = grad_out.shape[1]
    outer_len = rows_dev * devices
    seq_len = outer_len * inner_len
    cols_dev = inner_len // devices
    freq_dev = input_spec.shape[1]
    inv_total = 1.0 / seq_len
    inv_root = 1.0 / math.sqrt(seq_len)
    cosine_outer, sine_outer = cos_sin(outer_len)
    cosine_inner, sine_inner = cos_sin(inner_len)
    my_rows = my_index * rows_dev + jnp.arange(rows_dev, dtype=jnp.int32)
    row_positions = (
        my_rows[:, None] * inner_len + jnp.arange(inner_len, dtype=jnp.int32)[None, :]
    ).astype(jnp.float32) * inv_total
    columns = lax.all_to_all(grad_out, "outer", split_axis=1, concat_axis=0, tiled=True)
    part_real = outer_section(cosine_outer, columns)
    part_imag = -outer_section(sine_outer, columns)
    my_cols = my_index * cols_dev + jnp.arange(cols_dev, dtype=jnp.int32)
    twist_cos, twist_sin = twiddle(jnp.arange(outer_len, dtype=jnp.int32), my_cols, seq_len)
    shifted_real = (part_real * twist_cos + part_imag * twist_sin).astype(jnp.bfloat16)
    shifted_imag = (part_imag * twist_cos - part_real * twist_sin).astype(jnp.bfloat16)
    freq_real, freq_imag = (
        lax.all_to_all(shifted_real, "outer", split_axis=0, concat_axis=1, tiled=True),
        lax.all_to_all(shifted_imag, "outer", split_axis=0, concat_axis=1, tiled=True),
    )
    spec_real = inner_section(freq_real, cosine_inner) + inner_section(freq_imag, sine_inner)
    spec_imag = inner_section(freq_imag, cosine_inner) - inner_section(freq_real, sine_inner)
    my_freq = my_index * freq_dev + jnp.arange(freq_dev, dtype=jnp.int32)
    back_cos, back_sin = twiddle(my_freq, jnp.arange(inner_len, dtype=jnp.int32), seq_len)

    def correlate(spectrum):
        real_part = spectrum[0].astype(jnp.float32)
        imag_part = spectrum[1].astype(jnp.float32)
        return (
            (real_part * spec_real + imag_part * spec_imag).astype(jnp.bfloat16),
            (real_part * spec_imag - imag_part * spec_real).astype(jnp.bfloat16),
        )

    def inverse_inner(halves):
        real_part, imag_part = halves
        mixed_real = inner_section(real_part, cosine_inner) - inner_section(imag_part, sine_inner)
        mixed_imag = inner_section(imag_part, cosine_inner) + inner_section(real_part, sine_inner)
        return (
            (mixed_real * back_cos - mixed_imag * back_sin).astype(jnp.bfloat16),
            (mixed_imag * back_cos + mixed_real * back_sin).astype(jnp.bfloat16),
        )

    def last_section(real_part, imag_part):
        summed = outer_section(cosine_outer, real_part) - outer_section(sine_outer, imag_part)
        return (summed * inv_total).astype(jnp.bfloat16)

    def one_last(halves):
        return last_section(halves[0], halves[1])

    input_turned = inverse_inner(correlate(kernel_spec))
    grad_cols = one_last(
        (
            lax.all_to_all(input_turned[0], "outer", split_axis=1, concat_axis=0, tiled=True),
            lax.all_to_all(input_turned[1], "outer", split_axis=1, concat_axis=0, tiled=True),
        )
    )
    kernel_turned = inverse_inner(correlate(input_spec))
    kern_cols = one_last(
        (
            lax.all_to_all(kernel_turned[0], "outer", split_axis=1, concat_axis=0, tiled=True),
            lax.all_to_all(kernel_turned[1], "outer", split_axis=1, concat_axis=0, tiled=True),
        )
    )
    grad_rows, kern_here = (
        lax.all_to_all(grad_cols, "outer", split_axis=0, concat_axis=1, tiled=True),
        lax.all_to_all(kern_cols, "outer", split_axis=0, concat_axis=1, tiled=True),
    )
    kernel_values = kern_here.astype(jnp.float32)
    window = jnp.exp(-decay * row_positions[:, :, None])
    raw_filter = jnp.einsum(
        "abf,fh->abh", filter_hidden, filter_w, preferred_element_type=jnp.float32
    )
    scaled = (kernel_values * window * inv_root).astype(jnp.bfloat16)
    weight_part = jnp.einsum(
        "abf,abh->fh", filter_hidden, scaled, preferred_element_type=jnp.float32
    )
    decay_part = (
        -jnp.sum(row_positions[:, :, None] * window * raw_filter * kernel_values, axis=(0, 1))
        * inv_root
    )
    grad_filter_w, grad_decay = lax.psum((weight_part, decay_part), "outer")
    return (grad_rows, grad_filter_w, grad_decay)


def turns(first_numbers, second_numbers, seq_len):
    product = first_numbers[:, None] * second_numbers[None, :] % seq_len
    angles = product.astype(jnp.float32) * (2.0 * math.pi / seq_len)
    cosine, sine = lax.optimization_barrier((jnp.cos(angles), jnp.sin(angles)))
    return (cosine[:, :, None], sine[:, :, None])


def dot(matrix, values):
    return jnp.dot(matrix, values, preferred_element_type=jnp.float32)


def beside(blocks):
    return jnp.concatenate(blocks, axis=1)


def call(kernel, grid, in_specs, out_specs, out_shape, flops, moved, *operands):
    return pl.pallas_call(
        kernel,
        grid=(grid,),
        in_specs=in_specs,
        out_specs=out_specs,
        out_shape=out_shape,
        compiler_params=pltpu.CompilerParams(
            dimension_semantics=("arbitrary",), vmem_limit_bytes=VMEM_BYTES
        ),
        cost_estimate=pl.CostEstimate(flops=flops, bytes_accessed=moved, transcendentals=0),
    )(*operands)


def whole(array):
    zeros = (0,) * array.ndim
    return pl.BlockSpec(array.shape, lambda step: zeros)


def block(array, axis, size):
    shape = array.shape[:axis] + (size,) + array.shape[axis + 1 :]
    return pl.BlockSpec(
        shape, lambda step: tuple(step if at == axis else 0 for at in range(len(shape)))
    )


def outer_forward_kernel(cos_ref, sin_ref, tc_ref, ts_ref, x_ref, real_ref, imag_ref):
    lanes = x_ref.shape[-1]
    values = beside([x_ref[:, k].reshape(-1, lanes) for k in range(PAIR)])
    real = dot(cos_ref[...], values)
    imag = -dot(sin_ref[...], values)
    for k in range(PAIR):
        r = real[:, k * lanes : (k + 1) * lanes]
        i = imag[:, k * lanes : (k + 1) * lanes]
        real_ref[k] = (r * tc_ref[k] + i * ts_ref[k]).astype(jnp.bfloat16)
        imag_ref[k] = (i * tc_ref[k] - r * ts_ref[k]).astype(jnp.bfloat16)


def inner_kernel(cos_ref, sin_ref, tc_ref, ts_ref, fr_ref, fi_ref, s_ref, real_ref, imag_ref):
    lanes = fr_ref.shape[-1]
    cosine, sine = cos_ref[...], sin_ref[...]
    in_real = beside([fr_ref[:, k].reshape(-1, lanes) for k in range(ROWS)])
    in_imag = beside([fi_ref[:, k].reshape(-1, lanes) for k in range(ROWS)])
    spec_real = dot(cosine, in_real) + dot(sine, in_imag)
    spec_imag = dot(cosine, in_imag) - dot(sine, in_real)
    kept_real = beside([s_ref[0, k] for k in range(ROWS)]).astype(jnp.float32)
    kept_imag = beside([s_ref[1, k] for k in range(ROWS)]).astype(jnp.float32)
    corr_real = (kept_real * spec_real + kept_imag * spec_imag).astype(jnp.bfloat16)
    corr_imag = (kept_real * spec_imag - kept_imag * spec_real).astype(jnp.bfloat16)
    mixed_real = dot(cosine, corr_real) - dot(sine, corr_imag)
    mixed_imag = dot(cosine, corr_imag) + dot(sine, corr_real)
    out_shape = (real_ref.shape[0],) + real_ref.shape[2:]
    for k in range(ROWS):
        r = mixed_real[:, k * lanes : (k + 1) * lanes]
        i = mixed_imag[:, k * lanes : (k + 1) * lanes]
        turned_real = (r * tc_ref[k] - i * ts_ref[k]).astype(jnp.bfloat16)
        turned_imag = (i * tc_ref[k] + r * ts_ref[k]).astype(jnp.bfloat16)
        real_ref[:, k] = turned_real.reshape(out_shape)
        imag_ref[:, k] = turned_imag.reshape(out_shape)


def outer_inverse_kernel(inv_total, cos_ref, sin_ref, tr_ref, ti_ref, out_ref):
    lanes = tr_ref.shape[-1]
    real = beside([tr_ref[k] for k in range(PAIR)])
    imag = beside([ti_ref[k] for k in range(PAIR)])
    summed = (dot(cos_ref[...], real) - dot(sin_ref[...], imag)) * inv_total
    for k in range(PAIR):
        out_ref[k] = summed[:, k * lanes : (k + 1) * lanes].astype(jnp.bfloat16)


def filter_kernel(
    inner_len,
    inv_total,
    inv_root,
    first_ref,
    cos_ref,
    sin_ref,
    tr_ref,
    ti_ref,
    hidden_ref,
    w_ref,
    decay_ref,
    weight_ref,
    slope_ref,
):
    step = pl.program_id(0)

    @pl.when(step == 0)
    def _():
        weight_ref[...] = jnp.zeros_like(weight_ref)
        slope_ref[...] = jnp.zeros_like(slope_ref)

    lanes = tr_ref.shape[-1]
    real = beside([tr_ref[k] for k in range(PAIR)])
    imag = beside([ti_ref[k] for k in range(PAIR)])
    values = (dot(cos_ref[...], real) - dot(sin_ref[...], imag)) * inv_total
    shape = values.shape
    hidden = hidden_ref[:, 0].reshape(shape[0], hidden_ref.shape[-1])
    row = lax.broadcasted_iota(jnp.int32, shape, 0)
    lane = lax.broadcasted_iota(jnp.int32, shape, 1)
    column = first_ref[0] + PAIR * step + (lane >= lanes).astype(jnp.int32)
    position = (row * inner_len + column).astype(jnp.float32) * inv_total
    weighted = jnp.exp(-decay_ref[...] * position) * values
    raw_filter = dot(hidden, w_ref[...])
    slope = position * weighted * raw_filter
    slope_ref[...] += jnp.sum(slope.reshape(-1, 8, shape[1]), axis=0)
    scaled = (weighted * inv_root).astype(jnp.bfloat16)
    weight_ref[...] += lax.dot_general(
        hidden, scaled, (((0,), (0,)), ((), ())), preferred_element_type=jnp.float32
    )


def shards(grad_out, input_spec, kernel_spec, filter_hidden, filter_w, decay):
    devices = lax.axis_size("outer")
    my_index = lax.axis_index("outer")
    rows_dev, inner_len, lanes = grad_out.shape
    outer_len = rows_dev * devices
    seq_len = outer_len * inner_len
    cols_dev = inner_len // devices
    if rows_dev % 16 or cols_dev % 16 or devices % 2 or devices & (devices - 1):
        return plain_shards(
            grad_out, input_spec, kernel_spec, filter_hidden, filter_w, decay
        )
    freq_dev = input_spec.shape[1]
    half = devices // 2
    half_cols = inner_len // half
    half_len = freq_dev * half
    order = filter_hidden.shape[-1]
    inv_total = 1.0 / seq_len
    inv_root = 1.0 / math.sqrt(seq_len)
    groups = [list(range(half)), list(range(half, devices))]
    bf16 = functools.partial(jax.ShapeDtypeStruct, dtype=jnp.bfloat16)
    f32 = functools.partial(jax.ShapeDtypeStruct, dtype=jnp.float32)
    cosine_outer, sine_outer = cos_sin(outer_len)
    cosine_inner, sine_inner = cos_sin(inner_len)

    def exchange(values, axis_index_groups=None):
        return lax.all_to_all(
            values,
            "outer",
            split_axis=0,
            concat_axis=0,
            axis_index_groups=axis_index_groups,
            tiled=True,
        )

    columns = exchange(
        grad_out.reshape(rows_dev, devices, cols_dev, lanes).transpose(1, 2, 0, 3)
    )
    hidden = filter_hidden.reshape(rows_dev, half, half_cols // PAIR, PAIR * order)
    hidden = hidden.transpose(1, 2, 0, 3)
    hidden = jnp.concatenate((hidden, hidden), axis=0)
    middle = hidden.shape[1] // 2
    my_cols = my_index * cols_dev + jnp.arange(cols_dev, dtype=jnp.int32)
    twist_cos, twist_sin = turns(my_cols, jnp.arange(outer_len, dtype=jnp.int32), seq_len)
    my_freq = my_index * freq_dev + jnp.arange(freq_dev, dtype=jnp.int32)
    back_cos, back_sin = turns(my_freq, jnp.arange(inner_len, dtype=jnp.int32), seq_len)
    tables = (cosine_outer, sine_outer, cosine_inner, sine_inner)
    twists = (twist_cos, twist_sin, back_cos, back_sin)
    early_hidden, columns, tables, twists = lax.optimization_barrier(
        (hidden[:, :middle], columns, tables, twists)
    )
    cosine_outer, sine_outer, cosine_inner, sine_inner = tables
    twist_cos, twist_sin, back_cos, back_sin = twists
    early_hidden = exchange(early_hidden)

    table_bytes = 4 * outer_len * outer_len
    column_bytes = 2 * outer_len * cols_dev * lanes
    turn_bytes = 8 * 128 * outer_len * cols_dev
    outer_flops = 4 * outer_len * outer_len * cols_dev * lanes
    inner_flops = 16 * freq_dev * inner_len * inner_len * lanes
    shape = (cols_dev, outer_len, lanes)
    shifted = call(
        outer_forward_kernel,
        cols_dev // PAIR,
        [whole(cosine_outer), whole(sine_outer), block(twist_cos, 0, PAIR),
         block(twist_sin, 0, PAIR), block(columns, 1, PAIR)],
        [block(bf16(shape), 0, PAIR)] * 2,
        [bf16(shape)] * 2,
        outer_flops,
        table_bytes + 3 * column_bytes + turn_bytes,
        cosine_outer, sine_outer, twist_cos, twist_sin, columns,
    )
    shifted = [
        part.reshape(cols_dev, devices, freq_dev, lanes).transpose(1, 2, 0, 3)
        for part in shifted
    ]
    early_hidden, shifted = lax.optimization_barrier((early_hidden, shifted))
    freq_real, freq_imag = [exchange(part) for part in shifted]
    late_hidden, freq_real, freq_imag = lax.optimization_barrier(
        (hidden[:, middle:], freq_real, freq_imag)
    )
    late_hidden = exchange(late_hidden)

    def turned_of(spectrum, freq_real, freq_imag, pieces):
        shape = (pieces, freq_dev, inner_len // pieces, lanes)
        return call(
            inner_kernel,
            freq_dev // ROWS,
            [whole(cosine_inner), whole(sine_inner), block(back_cos, 0, ROWS),
             block(back_sin, 0, ROWS), block(freq_real, 1, ROWS), block(freq_imag, 1, ROWS),
             block(spectrum, 1, ROWS)],
            [block(bf16(shape), 1, ROWS)] * 2,
            [bf16(shape)] * 2,
            inner_flops,
            6 * column_bytes + turn_bytes,
            cosine_inner, sine_inner, back_cos, back_sin, freq_real, freq_imag, spectrum,
        )

    def by_column(part):
        return part.transpose(2, 0, 1, 3).reshape(part.shape[2], -1, lanes)

    input_turned = turned_of(kernel_spec, freq_real, freq_imag, devices)
    (freq_real, freq_imag), input_turned = lax.optimization_barrier(
        ((freq_real, freq_imag), input_turned)
    )
    kernel_turned = turned_of(input_spec, freq_real, freq_imag, half)
    late_hidden, input_turned = lax.optimization_barrier((late_hidden, input_turned))
    input_parts = [exchange(part) for part in input_turned]
    kernel_turned, input_parts = lax.optimization_barrier((kernel_turned, input_parts))
    kernel_parts = [exchange(part, groups) for part in kernel_turned]
    input_parts = [by_column(part) for part in input_parts]

    grad_cols = call(
        functools.partial(outer_inverse_kernel, inv_total),
        cols_dev // PAIR,
        [whole(cosine_outer), whole(sine_outer)] + [block(input_parts[0], 0, PAIR)] * 2,
        block(bf16(shape), 0, PAIR),
        bf16(shape),
        outer_flops,
        table_bytes + 3 * column_bytes,
        cosine_outer, sine_outer, *input_parts,
    )
    grad_cols = grad_cols.reshape(cols_dev, devices, rows_dev, lanes).transpose(1, 2, 0, 3)
    kernel_parts, grad_cols = lax.optimization_barrier((kernel_parts, grad_cols))
    grad_rows = exchange(grad_cols).transpose(1, 0, 2, 3).reshape(grad_out.shape)

    kernel_parts = [by_column(part) for part in kernel_parts]
    half_at = my_index // half * half_len
    half_cos = lax.dynamic_slice_in_dim(cosine_outer, half_at, half_len, 1)
    half_sin = lax.dynamic_slice_in_dim(sine_outer, half_at, half_len, 1)
    first = (my_index % half * half_cols).astype(jnp.int32).reshape(1)
    hidden = jnp.concatenate((early_hidden, late_hidden), axis=1)
    nothing = jnp.zeros_like(filter_w)
    paired_w = jnp.concatenate(
        (
            jnp.concatenate((filter_w, nothing), axis=1),
            jnp.concatenate((nothing, filter_w), axis=1),
        ),
        axis=0,
    )
    paired_decay = jnp.concatenate((decay, decay))[None]
    weight_shape, slope_shape = (PAIR * order, PAIR * lanes), (8, PAIR * lanes)
    weight, slope = call(
        functools.partial(filter_kernel, inner_len, inv_total, inv_root),
        half_cols // PAIR,
        [pl.BlockSpec(memory_space=pltpu.SMEM), whole(half_cos), whole(half_sin),
         block(kernel_parts[0], 0, PAIR), block(kernel_parts[1], 0, PAIR), block(hidden, 1, 1),
         whole(paired_w), whole(paired_decay)],
        [whole(f32(weight_shape)), whole(f32(slope_shape))],
        [f32(weight_shape), f32(slope_shape)],
        outer_flops,
        table_bytes // 2 + 3 * column_bytes,
        first, half_cos, half_sin, *kernel_parts, hidden, paired_w, paired_decay,
    )
    weight = weight[:order, :lanes] + weight[order:, lanes:]
    slope = jnp.sum(slope[:, :lanes] + slope[:, lanes:], axis=0, keepdims=True)
    both = jnp.concatenate((weight, -slope * inv_root), axis=0)
    step = 1
    while step < devices:
        pairs = [(source, source ^ step) for source in range(devices)]
        both = both + lax.ppermute(both, "outer", pairs)
        step *= 2
    return (grad_rows, both[:order], both[order])


def solution(mesh):
    placed = (
        P(("grp", "outer"), None, None),
        P(None, ("grp", "outer"), None, None),
        P(None, "outer", None, None),
        P("outer", None, None),
        P(),
        P(),
    )
    return jax.shard_map(
        shards,
        mesh=mesh,
        in_specs=placed,
        out_specs=(P(("grp", "outer"), None, None), P("grp", None), P("grp")),
        check_vma=False,
    )
```
